32 devices in a mesh: groups: 2 (over x), gx: 4 (over y, core), gy: 4 (over z).
Axes of the slice: x: 2, y: 2, z: 4, core: 2. Of those that a mesh axis runs over, the one named last changes fastest.
Arguments:
- hidden: bfloat16 [16, 16384], P('groups', 'gx'), parts along dimension 0, may hold values from -6 to 6
- norm_gain: bfloat16 [16384], P('gx'), may hold values from 0.099609375 to 1.8984375
- w_qkv: bfloat16 [16384, 9216], P('gx', 'gy'), may hold values from -0.046875 to 0.046875
- w_out: bfloat16 [8192, 16384], P('gx', 'gy'), may hold values from -0.0625 to 0.0625
- cache_keys: bfloat16 [32, 4096, 512], P(('groups', 'gx', 'gy')), parts along dimension 0, may hold values from -250 to 250
- cache_values: bfloat16 [32, 4096, 512], P(('groups', 'gx', 'gy')), parts along dimension 0, may hold values from -6 to 6
- lengths: int32 [16], P('groups'), parts along dimension 0, may hold values from 512 to 4096, as said below
- owners: int32 [16], P('groups'), parts along dimension 0, may hold values from 0 to 15, as said below
Outputs:
- output: bfloat16 [16, 16384], P(('groups', 'gx'), 'gy'), parts along dimension 0
The draws below stay inside these ranges and needn't reach their ends.
There are 2 independent parts, one for each index of `groups`. The reference program is written for one: setup_inputs(seed, part) draws one part's arguments, and reference() takes and returns one part's arrays. A program takes and returns all parts, laid end to end along the dimension named above; an argument that names none is the same for every part. Nothing has to cross between parts.
Inputs may be any that keep to these rules, and one draw needn't show every extreme that they name: `lengths`: each row's cached length; some row has exactly 4096. Distinct slot numbers: row r's cache is cache_keys[owners[r]] and cache_values[owners[r]].
All inputs are finite; a program needn't handle non-finite values.
Results may differ from the reference program's by a relative error of at most 0.0075.
The reference program's roundings to bfloat16 on the way count: a program that leaves them out, or rounds other values in their place, can miss the bound.
Values may be sent and summed in bfloat16 or wider, within the bound.
A program may use at most 128 MiB of HBM per device.

```python
import jax
import jax.numpy as jnp
from jax import lax

D = 16384
QH = 64
KVH = 4
HD = 128
CAP = 4096
SLOTS = 16
ROWS = 8
QKVW = 9216
ATT = 8192


def draw_lengths(key, part):
    key = jax.random.fold_in(key, 11)
    first_key, second_key = jax.random.split(key)
    drawn = jax.random.randint(first_key, (ROWS,), CAP // 8, CAP + 1).astype(jnp.int32)
    chosen = jax.random.randint(second_key, (), 0, ROWS)
    return drawn.at[chosen].set(CAP).astype(jnp.int32)


def draw_owners(key, part):
    key = jax.random.fold_in(key, 12)
    shuffled = jax.random.permutation(key, SLOTS)
    return shuffled[:ROWS].astype(jnp.int32)


def draw_cache_keys(key, part):
    key = jax.random.fold_in(key, 13)
    first_key = jax.random.fold_in(key, 0)
    shape_all = (SLOTS, CAP, KVH * HD)
    base_vals = jax.random.normal(first_key, shape_all, jnp.float32)
    return jnp.clip(base_vals, -6.0, 6.0).astype(jnp.bfloat16)


def block_levels(stream_key, shape, pieces, low, high):
    def one(axis_at, shards_of):
        steps = jax.random.uniform(jax.random.fold_in(jax.random.fold_in(stream_key, 6), axis_at), (shards_of,), jnp.float32, low / len(pieces), high / len(pieces))
        return jnp.repeat(jnp.exp(steps), shape[axis_at] // shards_of).reshape((-1,) + (1,) * (len(shape) - axis_at - 1))

    loudness = one(*pieces[0])
    for cut in pieces[1:]:
        loudness = loudness * one(*cut)
    return loudness


def normal_values(own_key, shape, scale, limit, cuts=(), kind=jnp.bfloat16):
    array = jax.random.normal(own_key, shape, jnp.float32) * scale
    if len(cuts) > 0:
        array = block_levels(own_key, shape, cuts, -0.22, 0.18) * array
    return jnp.clip(array, min=-limit, max=limit).astype(kind)


def setup_inputs(seed: int = 0, part: int = 0) -> dict:
    key_of = jax.random.split(jax.random.key(seed), 9)
    part_splits = jax.random.split(jax.random.fold_in(key_of[8], part), 9)
    return {
        "hidden": normal_values(part_splits[0], (ROWS, D), 1.0, 6.0, ((1, 4),)),
        "norm_gain": jnp.clip(1.0 + 0.18 * jax.random.normal(key_of[1], (D,), jnp.float32), 0.099609375, 1.8984375).astype(jnp.bfloat16),
        "w_qkv": normal_values(key_of[2], (D, QKVW), D ** -0.5, 0.046875, ((0, 4), (1, 4))),
        "w_out": normal_values(key_of[3], (ATT, D), ATT ** -0.5, 0.0625, ((0, 4), (1, 4))),
        "cache_keys": draw_cache_keys(jax.random.fold_in(jax.random.fold_in(key_of[8], part), 71), part),
        "cache_values": normal_values(part_splits[5], (SLOTS, CAP, KVH * HD), 1.0, 6.0, ((0, 16),)),
        "lengths": draw_lengths(jax.random.fold_in(jax.random.fold_in(key_of[8], part), 71), part),
        "owners": draw_owners(jax.random.fold_in(jax.random.fold_in(key_of[8], part), 71), part),
    }


ROPE_BASE = 500000.0
EPSILON = 1e-05

def rotate(columns, position):
    half_width = columns.shape[-1] // 2
    frequency = ROPE_BASE ** (-jnp.arange(half_width, dtype=jnp.float32) * 2.0 / columns.shape[-1])
    angles = position[..., None] * frequency
    cosine = jnp.cos(angles)
    sine = jnp.sin(angles)
    first = columns[..., :half_width]
    second = columns[..., half_width:]
    return jnp.concatenate([first * cosine - second * sine, first * sine + second * cosine], axis=-1)

def attend_row(query, key_new, value_new, keys, values, length):
    groups = QH // KVH
    scale_factor = HD ** (-0.5)
    query_grp = query.astype(jnp.float32).reshape(KVH, groups, HD)
    key_table = keys.astype(jnp.float32).reshape(-1, KVH, HD)
    value_table = values.astype(jnp.float32).reshape(-1, KVH, HD)
    scores = jnp.einsum('ghd,tgd->ght', query_grp, key_table) * scale_factor
    spots = jnp.arange(key_table.shape[0], dtype=jnp.int32)
    scores = jnp.where(spots[None, None, :] < length, scores, -jnp.inf)
    own_score = jnp.einsum('ghd,gd->gh', query_grp, key_new.astype(jnp.float32)) * scale_factor
    highest = jnp.maximum(lax.optimization_barrier(jnp.max(scores, axis=-1)), own_score)
    probs = jnp.exp(scores - highest[..., None])
    own_prob = jnp.exp(own_score - highest)
    total = lax.optimization_barrier(jnp.sum(probs, axis=-1)) + own_prob
    probs_low = lax.optimization_barrier(probs.astype(jnp.bfloat16)).astype(jnp.float32)
    own_low = lax.optimization_barrier(own_prob.astype(jnp.bfloat16)).astype(jnp.float32)
    summed = jnp.einsum('ght,tgd->ghd', probs_low, value_table)
    summed = summed + own_low[..., None] * value_new.astype(jnp.float32)[:, None, :]
    return (summed / total[..., None]).reshape(-1).astype(jnp.bfloat16)

def reference(hidden, norm_gain, w_qkv, w_out, cache_keys, cache_values, lengths, owners):
    floats = hidden.astype(jnp.float32)
    squares = lax.optimization_barrier(jnp.sum(floats * floats, axis=1))
    normed = (floats * lax.rsqrt(squares / D + EPSILON)[:, None] * norm_gain.astype(jnp.float32)).astype(jnp.bfloat16)
    projected = jnp.dot(normed, w_qkv, preferred_element_type=jnp.float32)
    heads = projected.reshape(ROWS, QH + 2 * KVH, HD)
    position = lengths.astype(jnp.float32)[:, None]
    rotated = jnp.concatenate([rotate(heads[:, :QH + KVH], position), heads[:, QH + KVH:]], axis=1).astype(jnp.bfloat16)

    def one_row(inputs):
        row_heads, slot_index, length = inputs
        return attend_row(row_heads[:QH], row_heads[QH:QH + KVH], row_heads[QH + KVH:], cache_keys[slot_index], cache_values[slot_index], length)
    attended = lax.map(one_row, (rotated, owners, lengths))
    return jnp.dot(attended, w_out, preferred_element_type=jnp.float32).astype(jnp.bfloat16)
```

```python
import functools

import jax
import jax.numpy as jnp
import numpy as np
from jax import lax
from jax.experimental import pallas as pl
from jax.experimental.pallas import tpu as pltpu
from jax.sharding import PartitionSpec as P

D = 16384
QH = 64
KVH = 4
HD = 128
GROUP = QH // KVH
HEADS = QH + 2 * KVH

ROPE_BASE = 500000.0
EPSILON = 1e-05
MESH = pl.DeviceIdType.MESH
F32 = jnp.float32
BF16 = jnp.bfloat16


def chunks_of(heads):
    for count in (3, 2):
        if heads % count == 0:
            return count
    return 1


def kernel(
    ngx, ngy, nc, no,
    lengths, owners, freq_ref, owner_row, hidden_ref, gain_ref, w_qkv, w_out, keys, values,
    out_ref,
    wq, wo, kt, vt, x_ref, normed, sq, send1, recv1, heads, qbd, scores, send3, recv3, lhs, part, recv5,
    w_sem, kv_sem, o_sem,
    sq_send, sq_recv, s1_send, s1_recv, s3_send, s3_recv, s5_send, s5_recv,
):
    rows = hidden_ref.shape[0]
    feats = hidden_ref.shape[1]
    slots = ngx * ngy
    group = lax.axis_index("groups")
    gx = lax.axis_index("gx")
    gy = lax.axis_index("gy")
    me = gx * ngy + gy
    hpc = recv1.shape[2]
    cw = hpc * HD
    here = nc * hpc
    cap = kt.shape[0]
    hpg = recv3.shape[1]
    ow = wo.shape[2]
    block = rows // ngx

    w_copies = [
        pltpu.make_async_copy(w_qkv.at[:, pl.ds(c * cw, cw)], wq.at[c], w_sem.at[c]) for c in range(nc)
    ]
    kv_copies = [
        pltpu.make_async_copy(keys.at[0], kt, kv_sem.at[0]),
        pltpu.make_async_copy(values.at[0], vt, kv_sem.at[1]),
    ]
    o_copies = [
        pltpu.make_async_copy(w_out.at[:, pl.ds(c * ow, ow)], wo.at[c], o_sem.at[c]) for c in range(no)
    ]
    for copy in w_copies:
        copy.start()

    def peer(d):
        other = lax.rem(me + d, slots)
        return other, (group, other // ngy, lax.rem(other, ngy))

    def peer_x(d):
        other = lax.rem(gx + d, ngx)
        return other, (group, other, gy)

    barrier = pltpu.get_barrier_semaphore()

    @pl.loop(1, slots)
    def _(d):
        _, target = peer(d)
        pl.semaphore_signal(barrier, inc=1, device_id=target, device_id_type=MESH)

    picker = (
        lax.broadcasted_iota(jnp.int32, (slots, rows), 0) == jnp.broadcast_to(owner_row[...], (slots, rows))
    ).astype(BF16)
    fc = min(feats, 1024)
    total = jnp.zeros((slots, 1), F32)
    for f in range(feats // fc):
        piece = jnp.dot(picker, hidden_ref[:, f * fc : (f + 1) * fc], preferred_element_type=F32)
        x_ref[:, f * fc : (f + 1) * fc] = piece
        total = total + jnp.sum(piece * piece, axis=1, keepdims=True)
    sq[gx] = jnp.broadcast_to(total, (slots, HD))

    pl.semaphore_wait(barrier, slots - 1)

    def sq_copy(d):
        other, target = peer_x(d)
        return pltpu.make_async_remote_copy(
            src_ref=sq.at[gx], dst_ref=sq.at[gx], send_sem=sq_send.at[d], recv_sem=sq_recv.at[d],
            device_id=target, device_id_type=MESH,
        )

    for d in range(1, ngx):
        sq_copy(d).start()
    for copy in kv_copies + o_copies:
        copy.start()

    length = jnp.int32(0)
    for r in range(rows):
        length = length + jnp.where(owners[r] == me, lengths[r], 0)
    angles = length.astype(F32) * freq_ref[...]
    cosine = jnp.cos(angles)
    sine = jnp.sin(angles)
    lane = lax.broadcasted_iota(jnp.int32, (1, HD), 1)
    signed = jnp.where(lane < HD // 2, -sine, sine)

    mix_shape = (hpg * rows, slots * hpg)
    at_row = lax.broadcasted_iota(jnp.int32, (hpg * rows, 1), 0)
    at_col = lax.broadcasted_iota(jnp.int32, (1, slots * hpg), 1)
    want_row = at_row & (rows - 1)
    owner_col = jnp.zeros((hpg * rows, 1), jnp.int32)
    for r in range(rows):
        owner_col = jnp.where(want_row == r, owners[r], owner_col)
    wanted = owner_col * hpg + at_row // rows
    lhs[...] = jnp.where(
        jnp.broadcast_to(wanted, mix_shape) == jnp.broadcast_to(at_col, mix_shape), 1.0, 0.0
    ).astype(BF16)

    for d in range(1, ngx):
        sq_copy(d).wait_recv()
    squares = sq[0]
    for i in range(1, ngx):
        squares = squares + sq[i]
    scale = lax.rsqrt(squares[:, :1] / D + EPSILON)
    for f in range(feats // fc):
        at = slice(f * fc, (f + 1) * fc)
        normed[:, at] = (x_ref[:, at] * scale * gain_ref[:, at].astype(F32)).astype(BF16)

    def s1_copy(c, d):
        other, target = peer(d)
        return pltpu.make_async_remote_copy(
            src_ref=send1.at[c, other], dst_ref=recv1.at[c, me], send_sem=s1_send.at[c, d],
            recv_sem=s1_recv.at[c, d], device_id=target, device_id_type=MESH,
        )

    kc = min(feats, 512)
    for c in range(nc):
        w_copies[c].wait()

        def step(k, acc):
            at = pl.ds(pl.multiple_of(k * kc, kc), kc)
            return acc + jnp.dot(normed[:, at], wq[c, at, :], preferred_element_type=F32)

        acc = lax.fori_loop(0, feats // kc, step, jnp.zeros((slots, cw), F32))
        for h in range(hpc):
            send1[c, :, h, :] = acc[:, h * HD : (h + 1) * HD]

        @pl.loop(1, slots)
        def _(d):
            s1_copy(c, d).start()

        recv1[c, me] = send1[c, me]

    for c in range(nc):

        @pl.loop(1, slots)
        def _(d):
            s1_copy(c, d).wait_recv()

        for y in range(ngy):
            piece = recv1[c, y]
            for i in range(1, ngx):
                piece = piece + recv1[c, i * ngy + y]
            heads[pl.ds(y * here + c * hpc, hpc), :] = piece
    turning = heads[: QH + KVH, :]
    turned = (turning * cosine + pltpu.roll(turning, HD // 2, 1) * signed).astype(BF16)
    query = turned[:QH, :].astype(F32)
    qbd[...] = jnp.zeros(qbd.shape, BF16)
    own = []
    value_new = []
    for g in range(KVH):
        at = slice(g * GROUP, (g + 1) * GROUP)
        qbd[at, g * HD : (g + 1) * HD] = turned[at, :]
        key_new = turned[QH + g : QH + g + 1, :].astype(F32)
        own.append(jnp.sum(query[at, :] * key_new, axis=1, keepdims=True))
        value_new.append(heads[QH + KVH + g : QH + KVH + g + 1, :].astype(BF16).astype(F32))
    own_score = jnp.concatenate(own, axis=0) * HD ** (-0.5)

    tc = min(cap, 512)
    kv_copies[0].wait()
    q = qbd[...]
    highest = own_score
    for t in range(cap // tc):
        s = lax.dot_general(
            q, kt[t * tc : (t + 1) * tc, :], (((1,), (1,)), ((), ())), preferred_element_type=F32
        ) * HD ** (-0.5)
        spot = t * tc + lax.broadcasted_iota(jnp.int32, (1, tc), 1)
        s = jnp.where(spot < length, s, -jnp.inf)
        scores[:, t * tc : (t + 1) * tc] = s
        highest = jnp.maximum(highest, jnp.max(s, axis=1, keepdims=True))
    kv_copies[1].wait()
    own_prob = jnp.exp(own_score - highest)
    total = own_prob
    summed = jnp.zeros((QH, KVH * HD), F32)
    for t in range(cap // tc):
        p = jnp.exp(scores[:, t * tc : (t + 1) * tc] - highest)
        total = total + jnp.sum(p, axis=1, keepdims=True)
        summed = summed + jnp.dot(p.astype(BF16), vt[t * tc : (t + 1) * tc, :], preferred_element_type=F32)
    own_low = own_prob.astype(BF16).astype(F32)
    for g in range(KVH):
        at = slice(g * GROUP, (g + 1) * GROUP)
        mine = summed[at, g * HD : (g + 1) * HD] + own_low[at, :] * value_new[g]
        mine = (mine / total[at, :]).astype(send3.dtype if send3.dtype == BF16 else BF16).astype(send3.dtype)
        for i in range(GROUP // hpg):
            send3[g * (GROUP // hpg) + i] = mine[i * hpg : (i + 1) * hpg, :]

    def s3_copy(d):
        other, target = peer(d)
        return pltpu.make_async_remote_copy(
            src_ref=send3.at[other // ngy], dst_ref=recv3.at[me], send_sem=s3_send.at[d],
            recv_sem=s3_recv.at[d], device_id=target, device_id_type=MESH,
        )

    @pl.loop(1, slots)
    def _(d):
        s3_copy(d).start()

    recv3[me] = send3[gx]

    @pl.loop(1, slots)
    def _(d):
        s3_copy(d).wait_recv()

    sent = recv3[...].reshape(slots * hpg, HD).astype(BF16)
    mixed = jnp.dot(lhs[...], sent, preferred_element_type=F32)
    for h in range(hpg):
        part[:, h * HD : (h + 1) * HD] = mixed[h * rows : (h + 1) * rows, :].astype(BF16)

    def s5_copy(c, d):
        other, target = peer_x(d)
        return pltpu.make_async_remote_copy(
            src_ref=recv5.at[1, c, other], dst_ref=recv5.at[0, c, gx], send_sem=s5_send.at[c, d],
            recv_sem=s5_recv.at[c, d], device_id=target, device_id_type=MESH,
        )

    depth = wo.shape[1]
    oc = min(depth, 512)
    for c in range(no):
        o_copies[c].wait()

        def step(k, acc):
            at = pl.ds(pl.multiple_of(k * oc, oc), oc)
            return acc + jnp.dot(part[:, at], wo[c, at, :], preferred_element_type=F32)

        acc = lax.fori_loop(0, depth // oc, step, jnp.zeros((rows, ow), F32))
        for i in range(ngx):
            recv5[1, c, i] = acc[i * block : (i + 1) * block, :]
        for d in range(1, ngx):
            s5_copy(c, d).start()
        recv5[0, c, gx] = recv5[1, c, gx]
    for c in range(no):
        for d in range(1, ngx):
            s5_copy(c, d).wait_recv()
        result = recv5[0, c, 0]
        for i in range(1, ngx):
            result = result + recv5[0, c, i]
        out_ref[:, c * ow : (c + 1) * ow] = result.astype(out_ref.dtype)

    for d in range(1, ngx):
        sq_copy(d).wait_send()
        for c in range(no):
            s5_copy(c, d).wait_send()

    @pl.loop(1, slots)
    def _(d):
        s3_copy(d).wait_send()
        for c in range(nc):
            s1_copy(c, d).wait_send()


def on_device(hidden, norm_gain, w_qkv, w_out, cache_keys, cache_values, lengths, owners):
    ngx = lax.axis_size("gx")
    ngy = lax.axis_size("gy")
    slots = ngx * ngy
    rows, feats = hidden.shape
    here = w_qkv.shape[1] // HD
    nc = chunks_of(here)
    hpc = here // nc
    hpg = w_out.shape[0] // HD
    no = 4
    ow = w_out.shape[1] // no
    cap = cache_keys.shape[1]
    half = HD // 2
    freq = np.float32(ROPE_BASE) ** (-np.arange(half, dtype=np.float32) * np.float32(2.0) / np.float32(HD))
    freq = jnp.asarray(np.concatenate([freq, freq])[None, :].astype(np.float32))
    sent = BF16 if hpg % 16 == 0 else F32
    dma = pltpu.SemaphoreType.DMA
    vmem = pl.BlockSpec(memory_space=pltpu.VMEM)
    smem = pl.BlockSpec(memory_space=pltpu.SMEM)
    hbm = pl.BlockSpec(memory_space=pl.ANY)
    return pl.pallas_call(
        functools.partial(kernel, ngx, ngy, nc, no),
        out_shape=jax.ShapeDtypeStruct((rows // ngx, w_out.shape[1]), BF16),
        in_specs=[smem, smem, vmem, vmem, vmem, vmem, hbm, hbm, hbm, hbm],
        out_specs=vmem,
        scratch_shapes=[
            pltpu.VMEM((nc, feats, hpc * HD), BF16),
            pltpu.VMEM((no, w_out.shape[0], ow), BF16),
            pltpu.VMEM((cap, KVH * HD), BF16),
            pltpu.VMEM((cap, KVH * HD), BF16),
            pltpu.VMEM((slots, feats), F32),
            pltpu.VMEM((slots, feats), BF16),
            pltpu.VMEM((ngx, slots, HD), F32),
            pltpu.VMEM((nc, slots, hpc, HD), F32),
            pltpu.VMEM((nc, slots, hpc, HD), F32),
            pltpu.VMEM((HEADS, HD), F32),
            pltpu.VMEM((QH, KVH * HD), BF16),
            pltpu.VMEM((QH, cap), F32),
            pltpu.VMEM((ngx, hpg, HD), sent),
            pltpu.VMEM((slots, hpg, HD), sent),
            pltpu.VMEM((hpg * rows, slots * hpg), BF16),
            pltpu.VMEM((rows, hpg * HD), BF16),
            pltpu.VMEM((2, no, ngx, rows // ngx, ow), F32),
            dma((nc,)), dma((2,)), dma((no,)),
            dma((ngx,)), dma((ngx,)),
            dma((nc, slots)), dma((nc, slots)),
            dma((slots,)), dma((slots,)),
            dma((no, ngx)), dma((no, ngx)),
        ],
        compiler_params=pltpu.CompilerParams(
            collective_id=0, has_side_effects=True, vmem_limit_bytes=56 * 1024 * 1024
        ),
        cost_estimate=pl.CostEstimate(flops=10**9, bytes_accessed=44 * 10**6, transcendentals=0),
    )(
        lengths, owners, freq, owners[None, :], hidden, norm_gain[None, :], w_qkv, w_out,
        cache_keys, cache_values,
    )


def solution(mesh):
    in_specs = (
        P("groups", "gx"),
        P("gx"),
        P("gx", "gy"),
        P("gx", "gy"),
        P(("groups", "gx", "gy"), None, None),
        P(("groups", "gx", "gy"), None, None),
        P("groups"),
        P("groups"),
    )
    out_specs = P(("groups", "gx"), "gy")
    return jax.shard_map(
        on_device, mesh=mesh, in_specs=in_specs, out_specs=out_specs, check_vma=False
    )
```

```python
import functools

import jax
import jax.numpy as jnp
import numpy as np
from jax import lax
from jax.experimental import pallas as pl
from jax.experimental.pallas import tpu as pltpu
from jax.sharding import PartitionSpec as P

D = 16384
QH = 64
KVH = 4
HD = 128
GROUP = QH // KVH
HEADS = QH + 2 * KVH

ROPE_BASE = 500000.0
EPSILON = 1e-05
MESH = pl.DeviceIdType.MESH
F32 = jnp.float32
BF16 = jnp.bfloat16


def chunks_of(heads):
    for count in (3, 2):
        if heads % count == 0:
            return count
    return 1


def kernel(
    ngx, ngy, nc, no,
    lengths, owners, freq, hidden, gain, w_qkv, w_out, keys, values,
    out_ref,
    freq_ref, hidden_ref, gain_ref,
    wq, wo, kt, vt, x_ref, normed, sq, send1, recv1, heads, qbd, scores, send3, recv3, lhs, part, recv5,
    in_sem, w_sem, kv_sem, o_sem,
    sq_send, sq_recv, s1_send, s1_recv, s3_send, s3_recv, s5_send, s5_recv,
):
    rows = hidden_ref.shape[0]
    feats = hidden_ref.shape[1]
    slots = ngx * ngy
    group = lax.axis_index("groups")
    gx = lax.axis_index("gx")
    gy = lax.axis_index("gy")
    me = gx * ngy + gy
    hpc = recv1.shape[2]
    cw = hpc * HD
    here = nc * hpc
    cap = kt.shape[0]
    hpg = recv3.shape[1]
    ow = wo.shape[2]
    block = rows // ngx

    hidden_copy = pltpu.make_async_copy(hidden, hidden_ref, in_sem.at[0])
    gain_copy = pltpu.make_async_copy(gain, gain_ref, in_sem.at[1])
    freq_copy = pltpu.make_async_copy(freq, freq_ref, in_sem.at[2])
    for copy in (hidden_copy, gain_copy, freq_copy):
        copy.start()
    w_copies = [
        pltpu.make_async_copy(w_qkv.at[:, pl.ds(c * cw, cw)], wq.at[c], w_sem.at[c]) for c in range(nc)
    ]
    kv_copies = [
        pltpu.make_async_copy(keys.at[0], kt, kv_sem.at[0]),
        pltpu.make_async_copy(values.at[0], vt, kv_sem.at[1]),
    ]
    o_copies = [
        pltpu.make_async_copy(w_out.at[:, pl.ds(c * ow, ow)], wo.at[c], o_sem.at[c]) for c in range(no)
    ]
    for copy in w_copies:
        copy.start()

    xs = [gx]
    for _ in range(ngx - 1):
        after = xs[-1] + 1
        xs.append(jnp.where(after == ngx, 0, after))
    ys = [gy]
    for _ in range(ngy - 1):
        after = ys[-1] + 1
        ys.append(jnp.where(after == ngy, 0, after))

    def peer_x(d):
        return xs[d], (group, xs[d], gy)

    few = slots <= 16

    def peer(d):
        if few:
            x, y = xs[d // ngy], ys[d % ngy]
        else:
            x, y = lax.rem(gx + d // ngy, ngx), lax.rem(gy + d % ngy, ngy)
        return x * ngy + y, x, (group, x, y)

    def each_peer(body):
        if few:
            for d in range(1, slots):
                body(d)
        else:

            @pl.loop(1, slots)
            def _(d):
                body(d)

    barrier = pltpu.get_barrier_semaphore()

    each_peer(lambda d: pl.semaphore_signal(barrier, inc=1, device_id=peer(d)[2], device_id_type=MESH))

    at_lane = lax.broadcasted_iota(jnp.int32, (slots, rows), 1)
    owner_of = jnp.zeros((slots, rows), jnp.int32)
    for r in range(rows):
        owner_of = jnp.where(at_lane == r, owners[r], owner_of)
    picker = jnp.where(lax.broadcasted_iota(jnp.int32, (slots, rows), 0) == owner_of, 1.0, 0.0).astype(BF16)
    hidden_copy.wait()
    fc = min(feats, 1024)
    total = jnp.zeros((slots, 1), F32)
    for f in range(feats // fc):
        piece = jnp.dot(picker, hidden_ref[:, f * fc : (f + 1) * fc], preferred_element_type=F32)
        x_ref[:, f * fc : (f + 1) * fc] = piece
        total = total + jnp.sum(piece * piece, axis=1, keepdims=True)
    sq[gx] = jnp.broadcast_to(total, (slots, HD))

    pl.semaphore_wait(barrier, slots - 1)

    def sq_copy(d):
        other, target = peer_x(d)
        return pltpu.make_async_remote_copy(
            src_ref=sq.at[gx], dst_ref=sq.at[gx], send_sem=sq_send.at[d], recv_sem=sq_recv.at[d],
            device_id=target, device_id_type=MESH,
        )

    for d in range(1, ngx):
        sq_copy(d).start()
    for copy in kv_copies + o_copies:
        copy.start()

    length = jnp.int32(0)
    for r in range(rows):
        length = length + jnp.where(owners[r] == me, lengths[r], 0)
    freq_copy.wait()
    angles = length.astype(F32) * freq_ref[...]
    cosine = jnp.cos(angles)
    sine = jnp.sin(angles)
    lane = lax.broadcasted_iota(jnp.int32, (1, HD), 1)
    signed = jnp.where(lane < HD // 2, -sine, sine)

    mix_shape = (hpg * rows, slots * hpg)
    at_row = lax.broadcasted_iota(jnp.int32, (hpg * rows, 1), 0)
    at_col = lax.broadcasted_iota(jnp.int32, (1, slots * hpg), 1)
    want_row = at_row & (rows - 1)
    owner_col = jnp.zeros((hpg * rows, 1), jnp.int32)
    for r in range(rows):
        owner_col = jnp.where(want_row == r, owners[r], owner_col)
    wanted = owner_col * hpg + at_row // rows
    lhs[...] = jnp.where(
        jnp.broadcast_to(wanted, mix_shape) == jnp.broadcast_to(at_col, mix_shape), 1.0, 0.0
    ).astype(BF16)

    gain_copy.wait()
    for d in range(1, ngx):
        sq_copy(d).wait_recv()
    squares = sq[0]
    for i in range(1, ngx):
        squares = squares + sq[i]
    scale = lax.rsqrt(squares[:, :1] / D + EPSILON)
    for f in range(feats // fc):
        at = slice(f * fc, (f + 1) * fc)
        normed[:, at] = (x_ref[:, at] * scale * jnp.broadcast_to(gain_ref[at].astype(F32), (slots, fc))).astype(BF16)

    def s1_copy(c, d):
        other, _, target = peer(d)
        return pltpu.make_async_remote_copy(
            src_ref=send1.at[c, other], dst_ref=recv1.at[c, me], send_sem=s1_send.at[c, d],
            recv_sem=s1_recv.at[c, d], device_id=target, device_id_type=MESH,
        )

    kc = min(feats, 512)
    for c in range(nc):
        w_copies[c].wait()

        def step(k, acc):
            at = pl.ds(pl.multiple_of(k * kc, kc), kc)
            return acc + jnp.dot(normed[:, at], wq[c, at, :], preferred_element_type=F32)

        acc = lax.fori_loop(0, feats // kc, step, jnp.zeros((slots, cw), F32))
        for h in range(hpc):
            send1[c, :, h, :] = acc[:, h * HD : (h + 1) * HD]

        each_peer(lambda d: s1_copy(c, d).start())

        recv1[c, me] = send1[c, me]

    for c in range(nc):
        each_peer(lambda d: s1_copy(c, d).wait_recv())

        for y in range(ngy):
            piece = recv1[c, y]
            for i in range(1, ngx):
                piece = piece + recv1[c, i * ngy + y]
            heads[pl.ds(y * here + c * hpc, hpc), :] = piece
    turning = heads[: QH + KVH, :]
    turned = (turning * cosine + pltpu.roll(turning, HD // 2, 1) * signed).astype(BF16)
    query = turned[:QH, :].astype(F32)
    qbd[...] = jnp.zeros(qbd.shape, BF16)
    own = []
    value_new = []
    for g in range(KVH):
        at = slice(g * GROUP, (g + 1) * GROUP)
        qbd[at, g * HD : (g + 1) * HD] = turned[at, :]
        key_new = turned[QH + g : QH + g + 1, :].astype(F32)
        own.append(jnp.sum(query[at, :] * key_new, axis=1, keepdims=True))
        value_new.append(heads[QH + KVH + g : QH + KVH + g + 1, :].astype(BF16).astype(F32))
    own_score = jnp.concatenate(own, axis=0) * HD ** (-0.5)

    tc = min(cap, 512)
    kv_copies[0].wait()
    q = qbd[...]
    highest = own_score
    for t in range(cap // tc):
        s = lax.dot_general(
            q, kt[t * tc : (t + 1) * tc, :], (((1,), (1,)), ((), ())), preferred_element_type=F32
        ) * HD ** (-0.5)
        spot = t * tc + lax.broadcasted_iota(jnp.int32, (1, tc), 1)
        s = jnp.where(spot < length, s, -jnp.inf)
        scores[:, t * tc : (t + 1) * tc] = s
        highest = jnp.maximum(highest, jnp.max(s, axis=1, keepdims=True))
    kv_copies[1].wait()
    own_prob = jnp.exp(own_score - highest)
    total = own_prob
    summed = jnp.zeros((QH, KVH * HD), F32)
    for t in range(cap // tc):
        p = jnp.exp(scores[:, t * tc : (t + 1) * tc] - highest)
        total = total + jnp.sum(p, axis=1, keepdims=True)
        summed = summed + jnp.dot(p.astype(BF16), vt[t * tc : (t + 1) * tc, :], preferred_element_type=F32)
    own_low = own_prob.astype(BF16).astype(F32)
    for g in range(KVH):
        at = slice(g * GROUP, (g + 1) * GROUP)
        mine = summed[at, g * HD : (g + 1) * HD] + own_low[at, :] * value_new[g]
        mine = (mine / total[at, :]).astype(BF16).astype(send3.dtype)
        for i in range(GROUP // hpg):
            send3[g * (GROUP // hpg) + i] = mine[i * hpg : (i + 1) * hpg, :]

    def s3_copy(d):
        _, x, target = peer(d)
        return pltpu.make_async_remote_copy(
            src_ref=send3.at[x], dst_ref=recv3.at[me], send_sem=s3_send.at[d],
            recv_sem=s3_recv.at[d], device_id=target, device_id_type=MESH,
        )

    each_peer(lambda d: s3_copy(d).start())

    recv3[me] = send3[gx]

    each_peer(lambda d: s3_copy(d).wait_recv())

    groups = recv3[...].reshape(slots * hpg, HD).astype(BF16)
    mixed = jnp.dot(lhs[...], groups, preferred_element_type=F32)
    for h in range(hpg):
        part[:, h * HD : (h + 1) * HD] = mixed[h * rows : (h + 1) * rows, :].astype(BF16)

    def s5_copy(c, d):
        other, target = peer_x(d)
        return pltpu.make_async_remote_copy(
            src_ref=recv5.at[1, c, other], dst_ref=recv5.at[0, c, gx], send_sem=s5_send.at[c, d],
            recv_sem=s5_recv.at[c, d], device_id=target, device_id_type=MESH,
        )

    depth = wo.shape[1]
    oc = min(depth, 512)
    for c in range(no):
        o_copies[c].wait()

        def step(k, acc):
            at = pl.ds(pl.multiple_of(k * oc, oc), oc)
            return acc + jnp.dot(part[:, at], wo[c, at, :], preferred_element_type=F32)

        acc = lax.fori_loop(0, depth // oc, step, jnp.zeros((rows, ow), F32))
        for i in range(ngx):
            recv5[1, c, i] = acc[i * block : (i + 1) * block, :]
        for d in range(1, ngx):
            s5_copy(c, d).start()
        recv5[0, c, gx] = recv5[1, c, gx]
    for c in range(no):
        for d in range(1, ngx):
            s5_copy(c, d).wait_recv()
        result = recv5[0, c, 0]
        for i in range(1, ngx):
            result = result + recv5[0, c, i]
        out_ref[:, c * ow : (c + 1) * ow] = result.astype(out_ref.dtype)

    for d in range(1, ngx):
        sq_copy(d).wait_send()
        for c in range(no):
            s5_copy(c, d).wait_send()

    def sent(d):
        s3_copy(d).wait_send()
        for c in range(nc):
            s1_copy(c, d).wait_send()

    each_peer(sent)


def on_device(hidden, norm_gain, w_qkv, w_out, cache_keys, cache_values, lengths, owners):
    ngx = lax.axis_size("gx")
    ngy = lax.axis_size("gy")
    slots = ngx * ngy
    rows, feats = hidden.shape
    here = w_qkv.shape[1] // HD
    nc = chunks_of(here)
    hpc = here // nc
    hpg = w_out.shape[0] // HD
    no = 4
    ow = w_out.shape[1] // no
    cap = cache_keys.shape[1]
    half = HD // 2
    freq = np.float32(ROPE_BASE) ** (-np.arange(half, dtype=np.float32) * np.float32(2.0) / np.float32(HD))
    freq = jnp.asarray(np.concatenate([freq, freq])[None, :].astype(np.float32))
    sent = BF16 if hpg % 16 == 0 else F32
    dma = pltpu.SemaphoreType.DMA
    vmem = pl.BlockSpec(memory_space=pltpu.VMEM)
    smem = pl.BlockSpec(memory_space=pltpu.SMEM)
    hbm = pl.BlockSpec(memory_space=pl.ANY)
    return pl.pallas_call(
        functools.partial(kernel, ngx, ngy, nc, no),
        out_shape=jax.ShapeDtypeStruct((rows // ngx, w_out.shape[1]), BF16),
        in_specs=[smem, smem, hbm, hbm, hbm, hbm, hbm, hbm, hbm],
        out_specs=vmem,
        scratch_shapes=[
            pltpu.VMEM((1, HD), F32),
            pltpu.VMEM((rows, feats), BF16),
            pltpu.VMEM((feats,), BF16),
            pltpu.VMEM((nc, feats, hpc * HD), BF16),
            pltpu.VMEM((no, w_out.shape[0], ow), BF16),
            pltpu.VMEM((cap, KVH * HD), BF16),
            pltpu.VMEM((cap, KVH * HD), BF16),
            pltpu.VMEM((slots, feats), F32),
            pltpu.VMEM((slots, feats), BF16),
            pltpu.VMEM((ngx, slots, HD), F32),
            pltpu.VMEM((nc, slots, hpc, HD), F32),
            pltpu.VMEM((nc, slots, hpc, HD), F32),
            pltpu.VMEM((HEADS, HD), F32),
            pltpu.VMEM((QH, KVH * HD), BF16),
            pltpu.VMEM((QH, cap), F32),
            pltpu.VMEM((ngx, hpg, HD), sent),
            pltpu.VMEM((slots, hpg, HD), sent),
            pltpu.VMEM((hpg * rows, slots * hpg), BF16),
            pltpu.VMEM((rows, hpg * HD), BF16),
            pltpu.VMEM((2, no, ngx, rows // ngx, ow), F32),
            dma((3,)), dma((nc,)), dma((2,)), dma((no,)),
            dma((ngx,)), dma((ngx,)),
            dma((nc, slots)), dma((nc, slots)),
            dma((slots,)), dma((slots,)),
            dma((no, ngx)), dma((no, ngx)),
        ],
        compiler_params=pltpu.CompilerParams(
            collective_id=0, has_side_effects=True, vmem_limit_bytes=56 * 1024 * 1024
        ),
        cost_estimate=pl.CostEstimate(flops=10**9, bytes_accessed=44 * 10**6, transcendentals=0),
    )(
        lengths, owners, freq, hidden, norm_gain, w_qkv, w_out,
        cache_keys, cache_values,
    )


def solution(mesh):
    in_specs = (
        P("groups", "gx"),
        P("gx"),
        P("gx", "gy"),
        P("gx", "gy"),
        P(("groups", "gx", "gy"), None, None),
        P(("groups", "gx", "gy"), None, None),
        P("groups"),
        P("groups"),
    )
    out_specs = P(("groups", "gx"), "gy")
    return jax.shard_map(
        on_device, mesh=mesh, in_specs=in_specs, out_specs=out_specs, check_vma=False
    )
```

```python
import functools

import jax
import jax.numpy as jnp
import numpy as np
from jax import lax
from jax.experimental import pallas as pl
from jax.experimental.pallas import tpu as pltpu
from jax.sharding import PartitionSpec as P

D = 16384
QH = 64
KVH = 4
HD = 128
GROUP = QH // KVH
HEADS = QH + 2 * KVH

ROPE_BASE = 500000.0
EPSILON = 1e-05
MESH = pl.DeviceIdType.MESH
F32 = jnp.float32
BF16 = jnp.bfloat16


def kernel(
    ngx, ngy, nc, no,
    lengths, owners, freq, hidden, gain, w_qkv, w_out, keys, values,
    out_ref,
    freq_ref, hidden_ref, gain_ref,
    wq, wo, kt, vt, x_ref, normed, sq, send1, recv1, heads, qbd, scores, send3, recv3, lhs, part, recv5,
    in_sem, w_sem, kv_sem, o_sem,
    sq_send, sq_recv, s1_send, s1_recv, s3_send, s3_recv, s5_send, s5_recv,
):
    rows = hidden_ref.shape[0]
    feats = hidden_ref.shape[1]
    slots = ngx * ngy
    group = lax.axis_index("groups")
    gx = lax.axis_index("gx")
    gy = lax.axis_index("gy")
    me = gx * ngy + gy
    hpc = recv1.shape[2]
    cw = hpc * HD
    here = nc * hpc
    cap = kt.shape[0]
    hpg = recv3.shape[1]
    ow = wo.shape[2]
    block = rows // ngx

    hidden_copy = pltpu.make_async_copy(hidden, hidden_ref, in_sem.at[0])
    gain_copy = pltpu.make_async_copy(gain, gain_ref, in_sem.at[1])
    freq_copy = pltpu.make_async_copy(freq, freq_ref, in_sem.at[2])
    for copy in (hidden_copy, gain_copy, freq_copy):
        copy.start()
    w_copies = [
        pltpu.make_async_copy(w_qkv.at[:, pl.ds(c * cw, cw)], wq.at[c], w_sem.at[c]) for c in range(nc)
    ]
    kv_copies = [
        pltpu.make_async_copy(keys.at[0], kt, kv_sem.at[0]),
        pltpu.make_async_copy(values.at[0], vt, kv_sem.at[1]),
    ]
    o_copies = [
        pltpu.make_async_copy(w_out.at[:, pl.ds(c * ow, ow)], wo.at[c], o_sem.at[c]) for c in range(no)
    ]
    for copy in w_copies:
        copy.start()

    xs = [gx]
    for _ in range(ngx - 1):
        after = xs[-1] + 1
        xs.append(jnp.where(after == ngx, 0, after))
    ys = [gy]
    for _ in range(ngy - 1):
        after = ys[-1] + 1
        ys.append(jnp.where(after == ngy, 0, after))

    def all_of(ref, count, semaphore):
        some = ref.at[pl.ds(0, count)]
        pltpu.make_async_copy(some, some, semaphore).wait()

    def peer_x(d):
        return xs[d], (group, xs[d], gy)

    few = slots <= 16

    def peer(d):
        if few:
            x, y = xs[d // ngy], ys[d % ngy]
        else:
            x, y = lax.rem(gx + d // ngy, ngx), lax.rem(gy + d % ngy, ngy)
        return x * ngy + y, x, (group, x, y)

    def each_peer(body):
        if few:
            for d in range(1, slots):
                body(d)
        else:

            @pl.loop(1, slots)
            def _(d):
                body(d)

    barrier = pltpu.get_barrier_semaphore()

    each_peer(lambda d: pl.semaphore_signal(barrier, inc=1, device_id=peer(d)[2], device_id_type=MESH))

    at_lane = lax.broadcasted_iota(jnp.int32, (slots, rows), 1)
    owner_of = jnp.zeros((slots, rows), jnp.int32)
    for r in range(rows):
        owner_of = jnp.where(at_lane == r, owners[r], owner_of)
    picker = jnp.where(lax.broadcasted_iota(jnp.int32, (slots, rows), 0) == owner_of, 1.0, 0.0).astype(BF16)
    hidden_copy.wait()
    fc = min(feats, 1024)
    total = jnp.zeros((slots, 1), F32)
    for f in range(feats // fc):
        piece = jnp.dot(picker, hidden_ref[:, f * fc : (f + 1) * fc], preferred_element_type=F32)
        x_ref[:, f * fc : (f + 1) * fc] = piece
        total = total + jnp.sum(piece * piece, axis=1, keepdims=True)
    sq[gx] = jnp.broadcast_to(total, (slots, HD))

    pl.semaphore_wait(barrier, slots - 1)

    def sq_copy(d):
        other, target = peer_x(d)
        return pltpu.make_async_remote_copy(
            src_ref=sq.at[gx], dst_ref=sq.at[gx], send_sem=sq_send, recv_sem=sq_recv,
            device_id=target, device_id_type=MESH,
        )

    for d in range(1, ngx):
        sq_copy(d).start()
    for copy in kv_copies + o_copies:
        copy.start()

    length = jnp.int32(0)
    for r in range(rows):
        length = length + jnp.where(owners[r] == me, lengths[r], 0)
    freq_copy.wait()
    angles = length.astype(F32) * freq_ref[...]
    cosine = jnp.cos(angles)
    sine = jnp.sin(angles)
    lane = lax.broadcasted_iota(jnp.int32, (1, HD), 1)
    signed = jnp.where(lane < HD // 2, -sine, sine)

    mix_shape = (hpg * rows, slots * hpg)
    at_row = lax.broadcasted_iota(jnp.int32, (hpg * rows, 1), 0)
    at_col = lax.broadcasted_iota(jnp.int32, (1, slots * hpg), 1)
    want_row = at_row & (rows - 1)
    owner_col = jnp.zeros((hpg * rows, 1), jnp.int32)
    for r in range(rows):
        owner_col = jnp.where(want_row == r, owners[r], owner_col)
    wanted = owner_col * hpg + at_row // rows
    lhs[...] = jnp.where(
        jnp.broadcast_to(wanted, mix_shape) == jnp.broadcast_to(at_col, mix_shape), 1.0, 0.0
    ).astype(BF16)

    gain_copy.wait()
    all_of(sq, ngx - 1, sq_recv)
    squares = sq[0]
    for i in range(1, ngx):
        squares = squares + sq[i]
    scale = lax.rsqrt(squares[:, :1] / D + EPSILON)
    for f in range(feats // fc):
        at = slice(f * fc, (f + 1) * fc)
        normed[:, at] = (x_ref[:, at] * scale * jnp.broadcast_to(gain_ref[at].astype(F32), (slots, fc))).astype(BF16)

    def s1_copy(c, d):
        other, _, target = peer(d)
        return pltpu.make_async_remote_copy(
            src_ref=send1.at[c, other], dst_ref=recv1.at[c, me], send_sem=s1_send.at[c],
            recv_sem=s1_recv.at[c], device_id=target, device_id_type=MESH,
        )

    kc = min(feats, 512)
    for c in range(nc):
        w_copies[c].wait()

        def step(k, acc):
            at = pl.ds(pl.multiple_of(k * kc, kc), kc)
            return acc + jnp.dot(normed[:, at], wq[c, at, :], preferred_element_type=F32)

        acc = lax.fori_loop(0, feats // kc, step, jnp.zeros((slots, cw), F32))
        for h in range(hpc):
            send1[c, :, h, :] = acc[:, h * HD : (h + 1) * HD]

        each_peer(lambda d: s1_copy(c, d).start())

        recv1[c, me] = send1[c, me]

    for c in range(nc):
        all_of(recv1.at[c], slots - 1, s1_recv.at[c])

        for y in range(ngy):
            piece = recv1[c, y]
            for i in range(1, ngx):
                piece = piece + recv1[c, i * ngy + y]
            heads[pl.ds(y * here + c * hpc, hpc), :] = piece
    turning = heads[: QH + KVH, :]
    turned = (turning * cosine + pltpu.roll(turning, HD // 2, 1) * signed).astype(BF16)
    query = turned[:QH, :].astype(F32)
    qbd[...] = jnp.zeros(qbd.shape, BF16)
    own = []
    value_new = []
    for g in range(KVH):
        at = slice(g * GROUP, (g + 1) * GROUP)
        qbd[at, g * HD : (g + 1) * HD] = turned[at, :]
        key_new = turned[QH + g : QH + g + 1, :].astype(F32)
        own.append(jnp.sum(query[at, :] * key_new, axis=1, keepdims=True))
        value_new.append(heads[QH + KVH + g : QH + KVH + g + 1, :].astype(BF16).astype(F32))
    own_score = jnp.concatenate(own, axis=0) * HD ** (-0.5)

    tc = min(cap, 512)
    kv_copies[0].wait()
    q = qbd[...]
    highest = own_score
    for t in range(cap // tc):
        s = lax.dot_general(
            q, kt[t * tc : (t + 1) * tc, :], (((1,), (1,)), ((), ())), preferred_element_type=F32
        ) * HD ** (-0.5)
        spot = t * tc + lax.broadcasted_iota(jnp.int32, (1, tc), 1)
        s = jnp.where(spot < length, s, -jnp.inf)
        scores[:, t * tc : (t + 1) * tc] = s
        highest = jnp.maximum(highest, jnp.max(s, axis=1, keepdims=True))
    kv_copies[1].wait()
    own_prob = jnp.exp(own_score - highest)
    total = own_prob
    summed = jnp.zeros((QH, KVH * HD), F32)
    for t in range(cap // tc):
        p = jnp.exp(scores[:, t * tc : (t + 1) * tc] - highest)
        total = total + jnp.sum(p, axis=1, keepdims=True)
        summed = summed + jnp.dot(p.astype(BF16), vt[t * tc : (t + 1) * tc, :], preferred_element_type=F32)
    own_low = own_prob.astype(BF16).astype(F32)
    for g in range(KVH):
        at = slice(g * GROUP, (g + 1) * GROUP)
        mine = summed[at, g * HD : (g + 1) * HD] + own_low[at, :] * value_new[g]
        mine = (mine / total[at, :]).astype(BF16).astype(send3.dtype)
        for i in range(GROUP // hpg):
            send3[g * (GROUP // hpg) + i] = mine[i * hpg : (i + 1) * hpg, :]

    def s3_copy(d):
        _, x, target = peer(d)
        return pltpu.make_async_remote_copy(
            src_ref=send3.at[x], dst_ref=recv3.at[me], send_sem=s3_send,
            recv_sem=s3_recv, device_id=target, device_id_type=MESH,
        )

    each_peer(lambda d: s3_copy(d).start())

    recv3[me] = send3[gx]

    all_of(sq, ngx - 1, sq_send)
    for c in range(nc):
        all_of(send1.at[c], slots - 1, s1_send.at[c])
    all_of(recv3, slots - 1, s3_recv)

    groups = recv3[...].reshape(slots * hpg, HD).astype(BF16)
    mixed = jnp.dot(lhs[...], groups, preferred_element_type=F32)
    for h in range(hpg):
        part[:, h * HD : (h + 1) * HD] = mixed[h * rows : (h + 1) * rows, :].astype(BF16)

    def s5_copy(c, d):
        other, target = peer_x(d)
        return pltpu.make_async_remote_copy(
            src_ref=recv5.at[1, c, other], dst_ref=recv5.at[0, c, gx], send_sem=s5_send.at[c],
            recv_sem=s5_recv.at[c], device_id=target, device_id_type=MESH,
        )

    depth = wo.shape[1]
    oc = min(depth, 512)
    for c in range(no):
        o_copies[c].wait()

        def step(k, acc):
            at = pl.ds(pl.multiple_of(k * oc, oc), oc)
            return acc + jnp.dot(part[:, at], wo[c, at, :], preferred_element_type=F32)

        acc = lax.fori_loop(0, depth // oc, step, jnp.zeros((rows, ow), F32))
        for i in range(ngx):
            recv5[1, c, i] = acc[i * block : (i + 1) * block, :]
        for d in range(1, ngx):
            s5_copy(c, d).start()
        recv5[0, c, gx] = recv5[1, c, gx]
    for c in range(no):
        if c == 0:
            all_of(recv3, slots - 1, s3_send)
        all_of(recv5.at[0, c], ngx - 1, s5_recv.at[c])
        result = recv5[0, c, 0]
        for i in range(1, ngx):
            result = result + recv5[0, c, i]
        out_ref[:, c * ow : (c + 1) * ow] = result.astype(out_ref.dtype)

    for c in range(no):
        all_of(recv5.at[0, c], ngx - 1, s5_send.at[c])


def on_device(hidden, norm_gain, w_qkv, w_out, cache_keys, cache_values, lengths, owners):
    ngx = lax.axis_size("gx")
    ngy = lax.axis_size("gy")
    slots = ngx * ngy
    rows, feats = hidden.shape
    here = w_qkv.shape[1] // HD
    nc = 1
    hpc = here // nc
    hpg = w_out.shape[0] // HD
    no = 1
    ow = w_out.shape[1] // no
    cap = cache_keys.shape[1]
    half = HD // 2
    freq = np.float32(ROPE_BASE) ** (-np.arange(half, dtype=np.float32) * np.float32(2.0) / np.float32(HD))
    freq = jnp.asarray(np.concatenate([freq, freq])[None, :].astype(np.float32))
    sent = BF16 if hpg % 16 == 0 else F32
    dma = pltpu.SemaphoreType.DMA
    vmem = pl.BlockSpec(memory_space=pltpu.VMEM)
    smem = pl.BlockSpec(memory_space=pltpu.SMEM)
    hbm = pl.BlockSpec(memory_space=pl.ANY)
    return pl.pallas_call(
        functools.partial(kernel, ngx, ngy, nc, no),
        out_shape=jax.ShapeDtypeStruct((rows // ngx, w_out.shape[1]), BF16),
        in_specs=[smem, smem, hbm, hbm, hbm, hbm, hbm, hbm, hbm],
        out_specs=vmem,
        scratch_shapes=[
            pltpu.VMEM((1, HD), F32),
            pltpu.VMEM((rows, feats), BF16),
            pltpu.VMEM((feats,), BF16),
            pltpu.VMEM((nc, feats, hpc * HD), BF16),
            pltpu.VMEM((no, w_out.shape[0], ow), BF16),
            pltpu.VMEM((cap, KVH * HD), BF16),
            pltpu.VMEM((cap, KVH * HD), BF16),
            pltpu.VMEM((slots, feats), F32),
            pltpu.VMEM((slots, feats), BF16),
            pltpu.VMEM((ngx, slots, HD), F32),
            pltpu.VMEM((nc, slots, hpc, HD), F32),
            pltpu.VMEM((nc, slots, hpc, HD), F32),
            pltpu.VMEM((HEADS, HD), F32),
            pltpu.VMEM((QH, KVH * HD), BF16),
            pltpu.VMEM((QH, cap), F32),
            pltpu.VMEM((ngx, hpg, HD), sent),
            pltpu.VMEM((slots, hpg, HD), sent),
            pltpu.VMEM((hpg * rows, slots * hpg), BF16),
            pltpu.VMEM((rows, hpg * HD), BF16),
            pltpu.VMEM((2, no, ngx, rows // ngx, ow), F32),
            dma((3,)), dma((nc,)), dma((2,)), dma((no,)),
            dma, dma,
            dma((nc,)), dma((nc,)),
            dma, dma,
            dma((no,)), dma((no,)),
        ],
        compiler_params=pltpu.CompilerParams(
            collective_id=0, has_side_effects=True, vmem_limit_bytes=56 * 1024 * 1024
        ),
        cost_estimate=pl.CostEstimate(flops=10**9, bytes_accessed=44 * 10**6, transcendentals=0),
    )(
        lengths, owners, freq, hidden, norm_gain, w_qkv, w_out,
        cache_keys, cache_values,
    )


def solution(mesh):
    in_specs = (
        P("groups", "gx"),
        P("gx"),
        P("gx", "gy"),
        P("gx", "gy"),
        P(("groups", "gx", "gy"), None, None),
        P(("groups", "gx", "gy"), None, None),
        P("groups"),
        P("groups"),
    )
    out_specs = P(("groups", "gx"), "gy")
    return jax.shard_map(
        on_device, mesh=mesh, in_specs=in_specs, out_specs=out_specs, check_vma=False
    )
```

```python
import functools

import jax
import jax.numpy as jnp
import numpy as np
from jax import lax
from jax.experimental import pallas as pl
from jax.experimental.pallas import tpu as pltpu
from jax.sharding import PartitionSpec as P

D = 16384
QH = 64
KVH = 4
HD = 128
GROUP = QH // KVH
HEADS = QH + 2 * KVH

ROPE_BASE = 500000.0
EPSILON = 1e-05
MESH = pl.DeviceIdType.MESH
F32 = jnp.float32
BF16 = jnp.bfloat16


def kernel(
    ngx, ngy, nc, no,
    lengths, owners, freq, hidden, gain, w_qkv, w_out, keys, values,
    out_ref,
    freq_ref, hidden_ref, gain_ref,
    wq, wo, kt, vt, x_ref, normed, sq, send1, recv1, heads, qbd, scores, send3, recv3, lhs, part, recv5,
    in_sem, w_sem, kv_sem, o_sem,
    sq_send, sq_recv, s1_send, s1_recv, s3_send, s3_recv, s5_send, s5_recv,
):
    rows = hidden_ref.shape[0]
    feats = hidden_ref.shape[1]
    slots = ngx * ngy
    group = lax.axis_index("groups")
    gx = lax.axis_index("gx")
    gy = lax.axis_index("gy")
    me = gx * ngy + gy
    hpc = recv1.shape[2]
    cw = hpc * HD
    here = nc * hpc
    cap = kt.shape[0]
    hpg = recv3.shape[1]
    ow = wo.shape[2]
    block = rows // ngx

    hidden_copy = pltpu.make_async_copy(hidden, hidden_ref, in_sem.at[0])
    gain_copy = pltpu.make_async_copy(gain, gain_ref, in_sem.at[1])
    freq_copy = pltpu.make_async_copy(freq, freq_ref, in_sem.at[2])
    for copy in (hidden_copy, gain_copy, freq_copy):
        copy.start()
    w_copies = [
        pltpu.make_async_copy(w_qkv.at[:, pl.ds(c * cw, cw)], wq.at[c], w_sem.at[c]) for c in range(nc)
    ]
    kv_copies = [
        pltpu.make_async_copy(keys.at[0], kt, kv_sem.at[0]),
        pltpu.make_async_copy(values.at[0], vt, kv_sem.at[1]),
    ]
    o_copies = [
        pltpu.make_async_copy(w_out.at[:, pl.ds(c * ow, ow)], wo.at[c], o_sem.at[c]) for c in range(no)
    ]
    for copy in w_copies:
        copy.start()

    xs = [gx]
    for _ in range(ngx - 1):
        after = xs[-1] + 1
        xs.append(jnp.where(after == ngx, 0, after))
    ys = [gy]
    for _ in range(ngy - 1):
        after = ys[-1] + 1
        ys.append(jnp.where(after == ngy, 0, after))

    def all_of(ref, count, semaphore):
        some = ref.at[pl.ds(0, count)]
        pltpu.make_async_copy(some, some, semaphore).wait()

    def peer_x(d):
        return xs[d], (group, xs[d], gy)

    few = slots <= 16

    def peer(d):
        if few:
            x, y = xs[d // ngy], ys[d % ngy]
        else:
            x, y = lax.rem(gx + d // ngy, ngx), lax.rem(gy + d % ngy, ngy)
        return x * ngy + y, x, (group, x, y)

    def each_peer(body):
        if few:
            for d in sorted(range(1, slots), key=lambda d: -(d % ngy) * ngx - d // ngy):
                body(d)
        else:

            @pl.loop(1, slots)
            def _(d):
                body(d)

    barrier = pltpu.get_barrier_semaphore()

    each_peer(lambda d: pl.semaphore_signal(barrier, inc=1, device_id=peer(d)[2], device_id_type=MESH))

    at_lane = lax.broadcasted_iota(jnp.int32, (slots, rows), 1)
    owner_of = jnp.zeros((slots, rows), jnp.int32)
    for r in range(rows):
        owner_of = jnp.where(at_lane == r, owners[r], owner_of)
    picker = jnp.where(lax.broadcasted_iota(jnp.int32, (slots, rows), 0) == owner_of, 1.0, 0.0).astype(BF16)
    hidden_copy.wait()
    fc = min(feats, 1024)
    total = jnp.zeros((slots, 1), F32)
    for f in range(feats // fc):
        piece = jnp.dot(picker, hidden_ref[:, f * fc : (f + 1) * fc], preferred_element_type=F32)
        x_ref[:, f * fc : (f + 1) * fc] = piece
        total = total + jnp.sum(piece * piece, axis=1, keepdims=True)
    sq[gx] = jnp.broadcast_to(total, (slots, HD))

    pl.semaphore_wait(barrier, slots - 1)

    def sq_copy(d):
        other, target = peer_x(d)
        return pltpu.make_async_remote_copy(
            src_ref=sq.at[gx], dst_ref=sq.at[gx], send_sem=sq_send, recv_sem=sq_recv,
            device_id=target, device_id_type=MESH,
        )

    for d in range(1, ngx):
        sq_copy(d).start()
    for copy in kv_copies + o_copies:
        copy.start()

    length = jnp.int32(0)
    for r in range(rows):
        length = length + jnp.where(owners[r] == me, lengths[r], 0)
    freq_copy.wait()
    angles = length.astype(F32) * freq_ref[...]
    cosine = jnp.cos(angles)
    sine = jnp.sin(angles)
    lane = lax.broadcasted_iota(jnp.int32, (1, HD), 1)
    signed = jnp.where(lane < HD // 2, -sine, sine)

    mix_shape = (hpg * rows, slots * hpg)
    at_row = lax.broadcasted_iota(jnp.int32, (hpg * rows, 1), 0)
    at_col = lax.broadcasted_iota(jnp.int32, (1, slots * hpg), 1)
    want_row = at_row & (rows - 1)
    owner_col = jnp.zeros((hpg * rows, 1), jnp.int32)
    for r in range(rows):
        owner_col = jnp.where(want_row == r, owners[r], owner_col)
    wanted = owner_col * hpg + at_row // rows
    lhs[...] = jnp.where(
        jnp.broadcast_to(wanted, mix_shape) == jnp.broadcast_to(at_col, mix_shape), 1.0, 0.0
    ).astype(BF16)

    gain_copy.wait()
    all_of(sq, ngx - 1, sq_recv)
    squares = sq[0]
    for i in range(1, ngx):
        squares = squares + sq[i]
    scale = lax.rsqrt(squares[:, :1] / D + EPSILON)
    for f in range(feats // fc):
        at = slice(f * fc, (f + 1) * fc)
        normed[:, at] = (x_ref[:, at] * scale * jnp.broadcast_to(gain_ref[at].astype(F32), (slots, fc))).astype(BF16)

    def s1_copy(c, d):
        other, _, target = peer(d)
        return pltpu.make_async_remote_copy(
            src_ref=send1.at[c, other], dst_ref=recv1.at[c, me], send_sem=s1_send.at[c],
            recv_sem=s1_recv.at[c], device_id=target, device_id_type=MESH,
        )

    kc = min(feats, 512)
    for c in range(nc):
        w_copies[c].wait()

        def step(k, acc):
            at = pl.ds(pl.multiple_of(k * kc, kc), kc)
            return acc + jnp.dot(normed[:, at], wq[c, at, :], preferred_element_type=F32)

        acc = lax.fori_loop(0, feats // kc, step, jnp.zeros((slots, cw), F32), unroll=True)
        for h in range(hpc):
            send1[c, :, h, :] = acc[:, h * HD : (h + 1) * HD]

        each_peer(lambda d: s1_copy(c, d).start())

        recv1[c, me] = send1[c, me]

    for c in range(nc):
        all_of(recv1.at[c], slots - 1, s1_recv.at[c])

        for y in range(ngy):
            piece = recv1[c, y]
            for i in range(1, ngx):
                piece = piece + recv1[c, i * ngy + y]
            heads[pl.ds(y * here + c * hpc, hpc), :] = piece
    turning = heads[: QH + KVH, :]
    turned = (turning * cosine + pltpu.roll(turning, HD // 2, 1) * signed).astype(BF16)
    query = turned[:QH, :].astype(F32)
    qbd[...] = jnp.zeros(qbd.shape, BF16)
    own = []
    value_new = []
    for g in range(KVH):
        at = slice(g * GROUP, (g + 1) * GROUP)
        qbd[at, g * HD : (g + 1) * HD] = turned[at, :]
        key_new = turned[QH + g : QH + g + 1, :].astype(F32)
        own.append(jnp.sum(query[at, :] * key_new, axis=1, keepdims=True))
        value_new.append(heads[QH + KVH + g : QH + KVH + g + 1, :].astype(BF16).astype(F32))
    own_score = jnp.concatenate(own, axis=0) * HD ** (-0.5)

    tc = min(cap, 512)
    kv_copies[0].wait()
    q = qbd[...]
    highest = own_score
    for t in range(cap // tc):
        s = lax.dot_general(
            q, kt[t * tc : (t + 1) * tc, :], (((1,), (1,)), ((), ())), preferred_element_type=F32
        ) * HD ** (-0.5)
        spot = t * tc + lax.broadcasted_iota(jnp.int32, (1, tc), 1)
        s = jnp.where(spot < length, s, -jnp.inf)
        scores[:, t * tc : (t + 1) * tc] = s
        highest = jnp.maximum(highest, jnp.max(s, axis=1, keepdims=True))
    kv_copies[1].wait()
    own_prob = jnp.exp(own_score - highest)
    total = own_prob
    summed = jnp.zeros((QH, KVH * HD), F32)
    for t in range(cap // tc):
        p = jnp.exp(scores[:, t * tc : (t + 1) * tc] - highest)
        total = total + jnp.sum(p, axis=1, keepdims=True)
        summed = summed + jnp.dot(p.astype(BF16), vt[t * tc : (t + 1) * tc, :], preferred_element_type=F32)
    own_low = own_prob.astype(BF16).astype(F32)
    for g in range(KVH):
        at = slice(g * GROUP, (g + 1) * GROUP)
        mine = summed[at, g * HD : (g + 1) * HD] + own_low[at, :] * value_new[g]
        mine = (mine / total[at, :]).astype(BF16).astype(send3.dtype)
        for i in range(GROUP // hpg):
            send3[g * (GROUP // hpg) + i] = mine[i * hpg : (i + 1) * hpg, :]

    def s3_copy(d):
        _, x, target = peer(d)
        return pltpu.make_async_remote_copy(
            src_ref=send3.at[x], dst_ref=recv3.at[me], send_sem=s3_send,
            recv_sem=s3_recv, device_id=target, device_id_type=MESH,
        )

    each_peer(lambda d: s3_copy(d).start())

    recv3[me] = send3[gx]

    all_of(sq, ngx - 1, sq_send)
    for c in range(nc):
        all_of(send1.at[c], slots - 1, s1_send.at[c])
    all_of(recv3, slots - 1, s3_recv)

    groups = recv3[...].reshape(slots * hpg, HD).astype(BF16)
    mixed = jnp.dot(lhs[...], groups, preferred_element_type=F32)
    for h in range(hpg):
        part[:, h * HD : (h + 1) * HD] = mixed[h * rows : (h + 1) * rows, :].astype(BF16)

    def s5_copy(c, d):
        other, target = peer_x(d)
        return pltpu.make_async_remote_copy(
            src_ref=recv5.at[1, c, other], dst_ref=recv5.at[0, c, gx], send_sem=s5_send.at[c],
            recv_sem=s5_recv.at[c], device_id=target, device_id_type=MESH,
        )

    depth = wo.shape[1]
    oc = min(depth, 512)
    for c in range(no):
        o_copies[c].wait()

        def step(k, acc):
            at = pl.ds(pl.multiple_of(k * oc, oc), oc)
            return acc + jnp.dot(part[:, at], wo[c, at, :], preferred_element_type=F32)

        acc = lax.fori_loop(0, depth // oc, step, jnp.zeros((rows, ow), F32), unroll=True)
        for i in range(ngx):
            recv5[1, c, i] = acc[i * block : (i + 1) * block, :]
        for d in range(1, ngx):
            s5_copy(c, d).start()
        recv5[0, c, gx] = recv5[1, c, gx]
    for c in range(no):
        if c == 0:
            all_of(recv3, slots - 1, s3_send)
        all_of(recv5.at[0, c], ngx - 1, s5_recv.at[c])
        result = recv5[0, c, 0]
        for i in range(1, ngx):
            result = result + recv5[0, c, i]
        out_ref[:, c * ow : (c + 1) * ow] = result.astype(out_ref.dtype)

    for c in range(no):
        all_of(recv5.at[0, c], ngx - 1, s5_send.at[c])


def on_device(hidden, norm_gain, w_qkv, w_out, cache_keys, cache_values, lengths, owners):
    ngx = lax.axis_size("gx")
    ngy = lax.axis_size("gy")
    slots = ngx * ngy
    rows, feats = hidden.shape
    here = w_qkv.shape[1] // HD
    nc = 1
    hpc = here // nc
    hpg = w_out.shape[0] // HD
    no = 1
    ow = w_out.shape[1] // no
    cap = cache_keys.shape[1]
    half = HD // 2
    freq = np.float32(ROPE_BASE) ** (-np.arange(half, dtype=np.float32) * np.float32(2.0) / np.float32(HD))
    freq = jnp.asarray(np.concatenate([freq, freq])[None, :].astype(np.float32))
    sent = BF16 if hpg % 16 == 0 else F32
    dma = pltpu.SemaphoreType.DMA
    vmem = pl.BlockSpec(memory_space=pltpu.VMEM)
    smem = pl.BlockSpec(memory_space=pltpu.SMEM)
    hbm = pl.BlockSpec(memory_space=pl.ANY)
    return pl.pallas_call(
        functools.partial(kernel, ngx, ngy, nc, no),
        out_shape=jax.ShapeDtypeStruct((rows // ngx, w_out.shape[1]), BF16),
        in_specs=[smem, smem, hbm, hbm, hbm, hbm, hbm, hbm, hbm],
        out_specs=vmem,
        scratch_shapes=[
            pltpu.VMEM((1, HD), F32),
            pltpu.VMEM((rows, feats), BF16),
            pltpu.VMEM((feats,), BF16),
            pltpu.VMEM((nc, feats, hpc * HD), BF16),
            pltpu.VMEM((no, w_out.shape[0], ow), BF16),
            pltpu.VMEM((cap, KVH * HD), BF16),
            pltpu.VMEM((cap, KVH * HD), BF16),
            pltpu.VMEM((slots, feats), F32),
            pltpu.VMEM((slots, feats), BF16),
            pltpu.VMEM((ngx, slots, HD), F32),
            pltpu.VMEM((nc, slots, hpc, HD), F32),
            pltpu.VMEM((nc, slots, hpc, HD), F32),
            pltpu.VMEM((HEADS, HD), F32),
            pltpu.VMEM((QH, KVH * HD), BF16),
            pltpu.VMEM((QH, cap), F32),
            pltpu.VMEM((ngx, hpg, HD), sent),
            pltpu.VMEM((slots, hpg, HD), sent),
            pltpu.VMEM((hpg * rows, slots * hpg), BF16),
            pltpu.VMEM((rows, hpg * HD), BF16),
            pltpu.VMEM((2, no, ngx, rows // ngx, ow), F32),
            dma((3,)), dma((nc,)), dma((2,)), dma((no,)),
            dma, dma,
            dma((nc,)), dma((nc,)),
            dma, dma,
            dma((no,)), dma((no,)),
        ],
        compiler_params=pltpu.CompilerParams(
            collective_id=0, has_side_effects=True, vmem_limit_bytes=56 * 1024 * 1024
        ),
        cost_estimate=pl.CostEstimate(flops=10**9, bytes_accessed=44 * 10**6, transcendentals=0),
    )(
        lengths, owners, freq, hidden, norm_gain, w_qkv, w_out,
        cache_keys, cache_values,
    )


def solution(mesh):
    in_specs = (
        P("groups", "gx"),
        P("gx"),
        P("gx", "gy"),
        P("gx", "gy"),
        P(("groups", "gx", "gy"), None, None),
        P(("groups", "gx", "gy"), None, None),
        P("groups"),
        P("groups"),
    )
    out_specs = P(("groups", "gx"), "gy")
    return jax.shard_map(
        on_device, mesh=mesh, in_specs=in_specs, out_specs=out_specs, check_vma=False
    )
```

```python
import functools

import jax
import jax.numpy as jnp
import numpy as np
from jax import lax
from jax.experimental import pallas as pl
from jax.experimental.pallas import tpu as pltpu
from jax.sharding import PartitionSpec as P

D = 16384
QH = 64
KVH = 4
HD = 128
GROUP = QH // KVH
HEADS = QH + 2 * KVH

ROPE_BASE = 500000.0
EPSILON = 1e-05
MESH = pl.DeviceIdType.MESH
F32 = jnp.float32
BF16 = jnp.bfloat16


def kernel(
    ngx, ngy, nc, no,
    lengths, owners, freq, hidden, gain, w_qkv, w_out, keys, values,
    out_ref,
    freq_ref, hidden_ref, gain_ref,
    wq, wo, kt, vt, x_ref, normed, sq, send1, recv1, heads, qbd, scores, send3, recv3, lhs, part, recv5,
    in_sem, w_sem, kv_sem, o_sem,
    sq_send, sq_recv, s1_send, s1_recv, s3_send, s3_recv, s5_send, s5_recv,
):
    rows = hidden_ref.shape[0]
    feats = hidden_ref.shape[1]
    slots = ngx * ngy
    group = lax.axis_index("groups")
    gx = lax.axis_index("gx")
    gy = lax.axis_index("gy")
    me = gx * ngy + gy
    hpc = recv1.shape[2]
    cw = hpc * HD
    here = nc * hpc
    cap = kt.shape[0]
    hpg = recv3.shape[1]
    ow = wo.shape[2]
    block = rows // ngx

    hidden_copy = pltpu.make_async_copy(hidden, hidden_ref, in_sem.at[0])
    gain_copy = pltpu.make_async_copy(gain, gain_ref, in_sem.at[1])
    freq_copy = pltpu.make_async_copy(freq, freq_ref, in_sem.at[2])
    for copy in (hidden_copy, gain_copy, freq_copy):
        copy.start()
    w_copies = [
        pltpu.make_async_copy(w_qkv.at[:, pl.ds(c * cw, cw)], wq.at[c], w_sem.at[c]) for c in range(nc)
    ]
    kv_copies = [
        pltpu.make_async_copy(keys.at[0], kt, kv_sem.at[0]),
        pltpu.make_async_copy(values.at[0], vt, kv_sem.at[1]),
    ]
    o_copies = [
        pltpu.make_async_copy(w_out.at[:, pl.ds(c * ow, ow)], wo.at[c], o_sem.at[c]) for c in range(no)
    ]
    for copy in w_copies:
        copy.start()

    xs = [gx]
    for _ in range(ngx - 1):
        after = xs[-1] + 1
        xs.append(jnp.where(after == ngx, 0, after))
    ys = [gy]
    for _ in range(ngy - 1):
        after = ys[-1] + 1
        ys.append(jnp.where(after == ngy, 0, after))

    def all_of(ref, count, semaphore):
        some = ref.at[pl.ds(0, count)]
        pltpu.make_async_copy(some, some, semaphore).wait()

    def peer_x(d):
        return xs[d], (group, xs[d], gy)

    few = slots <= 16

    def peer(d):
        if few:
            x, y = xs[d // ngy], ys[d % ngy]
        else:
            x, y = lax.rem(gx + d // ngy, ngx), lax.rem(gy + d % ngy, ngy)
        return x * ngy + y, x, (group, x, y)

    def each_peer(body):
        if few:
            for d in sorted(range(1, slots), key=lambda d: -(d % ngy) * ngx - d // ngy):
                body(d)
        else:

            @pl.loop(1, slots)
            def _(d):
                body(d)

    barrier = pltpu.get_barrier_semaphore()

    each_peer(lambda d: pl.semaphore_signal(barrier, inc=1, device_id=peer(d)[2], device_id_type=MESH))

    at_lane = lax.broadcasted_iota(jnp.int32, (slots, rows), 1)
    owner_of = jnp.zeros((slots, rows), jnp.int32)
    for r in range(rows):
        owner_of = jnp.where(at_lane == r, owners[r], owner_of)
    picker = jnp.where(lax.broadcasted_iota(jnp.int32, (slots, rows), 0) == owner_of, 1.0, 0.0).astype(BF16)
    hidden_copy.wait()
    fc = min(feats, 1024)
    total = jnp.zeros((slots, 1), F32)
    for f in range(feats // fc):
        piece = jnp.dot(picker, hidden_ref[:, f * fc : (f + 1) * fc], preferred_element_type=F32)
        x_ref[:, f * fc : (f + 1) * fc] = piece
        total = total + jnp.sum(piece * piece, axis=1, keepdims=True)
    sq[gx] = jnp.broadcast_to(total, (slots, HD))

    pl.semaphore_wait(barrier, slots - 1)

    def sq_copy(d):
        other, target = peer_x(d)
        return pltpu.make_async_remote_copy(
            src_ref=sq.at[gx], dst_ref=sq.at[gx], send_sem=sq_send, recv_sem=sq_recv,
            device_id=target, device_id_type=MESH,
        )

    for d in range(1, ngx):
        sq_copy(d).start()
    for copy in kv_copies + o_copies:
        copy.start()

    length = jnp.int32(0)
    for r in range(rows):
        length = length + jnp.where(owners[r] == me, lengths[r], 0)
    freq_copy.wait()
    angles = length.astype(F32) * freq_ref[...]
    cosine = jnp.cos(angles)
    sine = jnp.sin(angles)
    lane = lax.broadcasted_iota(jnp.int32, (1, HD), 1)
    signed = jnp.where(lane < HD // 2, -sine, sine)

    mix_shape = (hpg * rows, slots * hpg)
    at_row = lax.broadcasted_iota(jnp.int32, (hpg * rows, 1), 0)
    at_col = lax.broadcasted_iota(jnp.int32, (1, slots * hpg), 1)
    want_row = at_row & (rows - 1)
    owner_col = jnp.zeros((hpg * rows, 1), jnp.int32)
    for r in range(rows):
        owner_col = jnp.where(want_row == r, owners[r], owner_col)
    wanted = owner_col * hpg + at_row // rows
    lhs[...] = jnp.where(
        jnp.broadcast_to(wanted, mix_shape) == jnp.broadcast_to(at_col, mix_shape), 1.0, 0.0
    ).astype(BF16)

    gain_copy.wait()
    all_of(sq, ngx - 1, sq_recv)
    squares = sq[0]
    for i in range(1, ngx):
        squares = squares + sq[i]
    scale = lax.rsqrt(squares[:, :1] / D + EPSILON)
    for f in range(feats // fc):
        at = slice(f * fc, (f + 1) * fc)
        normed[:, at] = (x_ref[:, at] * scale * jnp.broadcast_to(gain_ref[at].astype(F32), (slots, fc))).astype(BF16)

    def s1_copy(c, d):
        other, _, target = peer(d)
        return pltpu.make_async_remote_copy(
            src_ref=send1.at[c, other], dst_ref=recv1.at[c, me], send_sem=s1_send.at[c],
            recv_sem=s1_recv.at[c], device_id=target, device_id_type=MESH,
        )

    kc = min(feats, 512)
    for c in range(nc):
        w_copies[c].wait()

        def step(k, acc):
            at = pl.ds(pl.multiple_of(k * kc, kc), kc)
            return acc + jnp.dot(normed[:, at], wq[c, at, :], preferred_element_type=F32)

        acc = lax.fori_loop(0, feats // kc, step, jnp.zeros((slots, cw), F32), unroll=True)
        for h in range(hpc):
            send1[c, :, h, :] = acc[:, h * HD : (h + 1) * HD]

        each_peer(lambda d: s1_copy(c, d).start())

        recv1[c, me] = send1[c, me]

    for c in range(nc):
        all_of(recv1.at[c], slots - 1, s1_recv.at[c])

        for y in range(ngy):
            piece = recv1[c, y]
            for i in range(1, ngx):
                piece = piece + recv1[c, i * ngy + y]
            heads[pl.ds(y * here + c * hpc, hpc), :] = piece
    turning = heads[: QH + KVH, :]
    turned = (turning * cosine + pltpu.roll(turning, HD // 2, 1) * signed).astype(BF16)
    query = turned[:QH, :].astype(F32)
    qbd[...] = jnp.zeros(qbd.shape, BF16)
    own = []
    value_new = []
    for g in range(KVH):
        at = slice(g * GROUP, (g + 1) * GROUP)
        qbd[at, g * HD : (g + 1) * HD] = turned[at, :]
        key_new = turned[QH + g : QH + g + 1, :].astype(F32)
        own.append(jnp.sum(query[at, :] * key_new, axis=1, keepdims=True))
        value_new.append(heads[QH + KVH + g : QH + KVH + g + 1, :].astype(BF16).astype(F32))
    own_score = jnp.concatenate(own, axis=0) * HD ** (-0.5)

    tc = min(cap, 512)
    kv_copies[0].wait()
    q = qbd[...]
    highest = own_score
    for t in range(cap // tc):
        s = lax.dot_general(
            q, kt[t * tc : (t + 1) * tc, :], (((1,), (1,)), ((), ())), preferred_element_type=F32
        ) * HD ** (-0.5)
        spot = t * tc + lax.broadcasted_iota(jnp.int32, (1, tc), 1)
        s = jnp.where(spot < length, s, -jnp.inf)
        scores[:, t * tc : (t + 1) * tc] = s
        highest = jnp.maximum(highest, jnp.max(s, axis=1, keepdims=True))
    kv_copies[1].wait()
    own_prob = jnp.exp(own_score - highest)
    total = own_prob
    summed = jnp.zeros((QH, KVH * HD), F32)
    for t in range(cap // tc):
        p = jnp.exp(scores[:, t * tc : (t + 1) * tc] - highest)
        total = total + jnp.sum(p, axis=1, keepdims=True)
        summed = summed + jnp.dot(p.astype(BF16), vt[t * tc : (t + 1) * tc, :], preferred_element_type=F32)
    own_low = own_prob.astype(BF16).astype(F32)
    for g in range(KVH):
        at = slice(g * GROUP, (g + 1) * GROUP)
        mine = summed[at, g * HD : (g + 1) * HD] + own_low[at, :] * value_new[g]
        mine = (mine / total[at, :]).astype(BF16).astype(send3.dtype)
        for i in range(GROUP // hpg):
            send3[g * (GROUP // hpg) + i] = mine[i * hpg : (i + 1) * hpg, :]

    def s3_copy(d):
        _, x, target = peer(d)
        return pltpu.make_async_remote_copy(
            src_ref=send3.at[x], dst_ref=recv3.at[me], send_sem=s3_send,
            recv_sem=s3_recv, device_id=target, device_id_type=MESH,
        )

    each_peer(lambda d: s3_copy(d).start())

    recv3[me] = send3[gx]

    all_of(sq, ngx - 1, sq_send)
    for c in range(nc):
        all_of(send1.at[c], slots - 1, s1_send.at[c])
    all_of(recv3, slots - 1, s3_recv)

    groups = recv3[...].reshape(slots * hpg, HD).astype(BF16)
    mixed = jnp.dot(lhs[...], groups, preferred_element_type=F32)
    for h in range(hpg):
        part[:, h * HD : (h + 1) * HD] = mixed[h * rows : (h + 1) * rows, :].astype(BF16)

    def s5_copy(c, d):
        other, target = peer_x(d)
        return pltpu.make_async_remote_copy(
            src_ref=recv5.at[1, c, other], dst_ref=recv5.at[0, c, gx], send_sem=s5_send.at[c],
            recv_sem=s5_recv.at[c], device_id=target, device_id_type=MESH,
        )

    depth = wo.shape[1]
    oc = min(depth, 512)
    for c in range(no):
        o_copies[c].wait()

        def step(k, acc):
            at = pl.ds(pl.multiple_of(k * oc, oc), oc)
            return acc + jnp.dot(part[:, at], wo[c, at, :], preferred_element_type=F32)

        acc = lax.fori_loop(0, depth // oc, step, jnp.zeros((rows, ow), F32), unroll=True)
        for i in range(ngx):
            recv5[1, c, i] = acc[i * block : (i + 1) * block, :]
        for d in range(1, ngx):
            s5_copy(c, d).start()
        recv5[0, c, gx] = recv5[1, c, gx]
    for c in range(no):
        if c == 0:
            all_of(recv3, slots - 1, s3_send)
        all_of(recv5.at[0, c], ngx - 1, s5_recv.at[c])
        result = recv5[0, c, 0]
        for i in range(1, ngx):
            result = result + recv5[0, c, i]
        out_ref[:, c * ow : (c + 1) * ow] = result.astype(out_ref.dtype)

    for c in range(no):
        all_of(recv5.at[0, c], ngx - 1, s5_send.at[c])


def on_device(hidden, norm_gain, w_qkv, w_out, cache_keys, cache_values, lengths, owners):
    ngx = lax.axis_size("gx")
    ngy = lax.axis_size("gy")
    slots = ngx * ngy
    rows, feats = hidden.shape
    here = w_qkv.shape[1] // HD
    nc = 2 if here % 2 == 0 else 1
    hpc = here // nc
    hpg = w_out.shape[0] // HD
    no = 1
    ow = w_out.shape[1] // no
    cap = cache_keys.shape[1]
    half = HD // 2
    freq = np.float32(ROPE_BASE) ** (-np.arange(half, dtype=np.float32) * np.float32(2.0) / np.float32(HD))
    freq = jnp.asarray(np.concatenate([freq, freq])[None, :].astype(np.float32))
    sent = BF16 if hpg % 16 == 0 else F32
    dma = pltpu.SemaphoreType.DMA
    vmem = pl.BlockSpec(memory_space=pltpu.VMEM)
    smem = pl.BlockSpec(memory_space=pltpu.SMEM)
    hbm = pl.BlockSpec(memory_space=pl.ANY)
    return pl.pallas_call(
        functools.partial(kernel, ngx, ngy, nc, no),
        out_shape=jax.ShapeDtypeStruct((rows // ngx, w_out.shape[1]), BF16),
        in_specs=[smem, smem, hbm, hbm, hbm, hbm, hbm, hbm, hbm],
        out_specs=vmem,
        scratch_shapes=[
            pltpu.VMEM((1, HD), F32),
            pltpu.VMEM((rows, feats), BF16),
            pltpu.VMEM((feats,), BF16),
            pltpu.VMEM((nc, feats, hpc * HD), BF16),
            pltpu.VMEM((no, w_out.shape[0], ow), BF16),
            pltpu.VMEM((cap, KVH * HD), BF16),
            pltpu.VMEM((cap, KVH * HD), BF16),
            pltpu.VMEM((slots, feats), F32),
            pltpu.VMEM((slots, feats), BF16),
            pltpu.VMEM((ngx, slots, HD), F32),
            pltpu.VMEM((nc, slots, hpc, HD), F32),
            pltpu.VMEM((nc, slots, hpc, HD), F32),
            pltpu.VMEM((HEADS, HD), F32),
            pltpu.VMEM((QH, KVH * HD), BF16),
            pltpu.VMEM((QH, cap), F32),
            pltpu.VMEM((ngx, hpg, HD), sent),
            pltpu.VMEM((slots, hpg, HD), sent),
            pltpu.VMEM((hpg * rows, slots * hpg), BF16),
            pltpu.VMEM((rows, hpg * HD), BF16),
            pltpu.VMEM((2, no, ngx, rows // ngx, ow), F32),
            dma((3,)), dma((nc,)), dma((2,)), dma((no,)),
            dma, dma,
            dma((nc,)), dma((nc,)),
            dma, dma,
            dma((no,)), dma((no,)),
        ],
        compiler_params=pltpu.CompilerParams(
            collective_id=0, has_side_effects=True, vmem_limit_bytes=56 * 1024 * 1024
        ),
        cost_estimate=pl.CostEstimate(flops=10**9, bytes_accessed=44 * 10**6, transcendentals=0),
    )(
        lengths, owners, freq, hidden, norm_gain, w_qkv, w_out,
        cache_keys, cache_values,
    )


def solution(mesh):
    in_specs = (
        P("groups", "gx"),
        P("gx"),
        P("gx", "gy"),
        P("gx", "gy"),
        P(("groups", "gx", "gy"), None, None),
        P(("groups", "gx", "gy"), None, None),
        P("groups"),
        P("groups"),
    )
    out_specs = P(("groups", "gx"), "gy")
    return jax.shard_map(
        on_device, mesh=mesh, in_specs=in_specs, out_specs=out_specs, check_vma=False
    )
```
